32 devices in a mesh: space: 8 (over z, y), param: 4 (over x, core).
Axes of the slice: x: 2, y: 2, z: 4, core: 2. Of those that a mesh axis runs over, the one named last changes fastest.
Arguments:
- snapshots: float32 [49152, 4096], P('space', 'param'), may hold values from -1800 to 1800
- sketch: float32 [4096, 32], P('param'), may hold values from -0.09375 to 0.09375
- sketch_next: float32 [256, 32], replicated, may hold values from -0.375 to 0.375
Outputs:
- first_core: float32 [32, 49152], P(None, 'space')
- second_core: float32 [32, 512], P(None, 'param')
- remainder: float32 [32, 256], replicated
The draws below stay inside these ranges and needn't reach their ends.
All inputs are finite; a program needn't handle non-finite values.
Results may differ from the reference program's by a relative error of at most 0.00016.
Values sent between devices are 32-bit elements; how exact they have to be, the bound alone decides.
No kernel may reach another device: no remote copies, remote signals or barrier semaphores. Data moves between devices by JAX's collectives and lax.ppermute only.
A program may use at most 128 MiB of HBM per device.

```python
import math
import jax
import jax.numpy as jnp
from jax import lax

R = 32
N1 = 16
N2 = 16
N3 = 16
ITERS = 3
C = 4096
ROWS = 49152


def draw_snapshots(key, part):
    key_values = jax.random.fold_in(key, 11)
    key_rows = jax.random.fold_in(key, 12)
    key_cols = jax.random.fold_in(key, 13)
    row_scale = jnp.exp(jax.random.uniform(key_rows, (ROWS, 1), jnp.float32) * math.log(10.0))
    ramp = 1.0 + 2.0 * jnp.arange(ROWS, dtype=jnp.float32)[:, None] / ROWS
    col_scale = jnp.exp(jax.random.uniform(key_cols, (1, C), jnp.float32) * math.log(10.0))
    values = jax.random.truncated_normal(key_values, -6.0, 6.0, (ROWS, C), jnp.float32)
    return (values * row_scale * ramp * col_scale).astype(jnp.float32)


def shard_levels(stream_key, extent, cuts, least, high):
    def one(position, blocks):
        steps = jax.random.uniform(jax.random.fold_in(jax.random.fold_in(stream_key, 6), position), (blocks,), jnp.float32, least / len(cuts), high / len(cuts))
        return jnp.repeat(jnp.exp(steps), extent[position] // blocks).reshape((-1,) + (1,) * (len(extent) - position - 1))

    loudness = one(*cuts[0])
    for cut in cuts[1:]:
        loudness = loudness * one(*cut)
    return loudness


def noise(rng, dims, spread, reach, pieces=(), kind=jnp.bfloat16):
    array = jax.random.normal(rng, dims, jnp.float32) * spread
    if len(pieces) > 0:
        array = shard_levels(rng, dims, pieces, -0.22, 0.18) * array
    return jnp.clip(array, min=-reach, max=reach).astype(kind)


def setup_inputs(seed: int = 0) -> dict:
    streams_of = jax.random.split(jax.random.key(seed), 4)
    return {
        "snapshots": draw_snapshots(jax.random.fold_in(streams_of[3], 71), 0),
        "sketch": noise(streams_of[1], (C, R), C ** -0.5, 0.09375, ((0, 4),), jnp.float32),
        "sketch_next": noise(streams_of[2], (N2 * N3, R), (N2 * N3) ** -0.5, 0.375, (), jnp.float32),
    }


def frame(block):
    highest = lax.Precision.HIGHEST
    gram_matrix = jnp.dot(block, block.T, precision=highest)
    lower = jnp.linalg.cholesky(gram_matrix)
    return jax.scipy.linalg.solve_triangular(lower, block, lower=True)

def reference(snapshots, sketch, sketch_next):
    highest = lax.Precision.HIGHEST
    sketched = lax.dot_general(sketch, snapshots, (((0,), (1,)), ((), ())), precision=highest)
    basis = frame(sketched)
    for step in range(ITERS):
        across = jnp.dot(basis, snapshots, precision=highest)
        column_frame = frame(across)
        sketched = lax.dot_general(column_frame, snapshots, (((1,), (1,)), ((), ())), precision=highest)
        basis = frame(sketched)
    coefficients = jnp.dot(basis, snapshots, precision=highest) / math.sqrt(ROWS)
    unfold = coefficients.reshape(R, N1, N2 * N3).transpose(1, 0, 2).reshape(N1 * R, N2 * N3)
    second_sketch = lax.dot_general(sketch_next, unfold, (((0,), (1,)), ((), ())), precision=highest)
    second_frame = frame(second_sketch)
    remainder = jnp.dot(second_frame, unfold, precision=highest) / math.sqrt(R * N1)
    return (basis * math.sqrt(ROWS), second_frame * math.sqrt(R * N1), remainder)
```

```python
import math

import jax
import jax.numpy as jnp
from jax import lax
from jax.experimental import pallas as pl
from jax.experimental.pallas import tpu as pltpu
from jax.sharding import PartitionSpec as P

R = 32
N2 = 16
N3 = 16
ITERS = 3
HIGHEST = lax.Precision.HIGHEST
F32 = jnp.float32
BF16 = jnp.bfloat16
LANES = 128
NT = (((1,), (1,)), ((), ()))


def split(block):
    high = block.astype(BF16)
    return high, (block - high.astype(F32)).astype(BF16)


def rows_kernel(frame_ref, a_ref, out_ref):
    frame_high, frame_low = split(frame_ref[...])
    both = jnp.concatenate([frame_high, frame_low], axis=0)
    high, low = split(a_ref[...])
    first = lax.dot_general(both, high, NT, preferred_element_type=F32)
    second = lax.dot_general(frame_high, low, NT, preferred_element_type=F32)
    out_ref[...] = first[:R] + (first[R:] + second)


def columns_kernel(s_ref, a_ref, out_ref):
    s = s_ref[...]
    s_high, s_low = split(s)
    both = jnp.concatenate([s_high, s_low], axis=0)
    high, low = split(a_ref[...])
    first = jnp.dot(both, high, preferred_element_type=F32)
    second = jnp.dot(s_high, low, preferred_element_type=F32)
    product = first[:R] + (first[R:] + second)
    gram = lax.dot_general(s, s, NT, precision=HIGHEST, preferred_element_type=F32)
    gram = jnp.concatenate([gram, jnp.zeros((R, LANES - R), F32)], axis=1)
    whole = jnp.concatenate([product, gram], axis=1)

    @pl.when(pl.program_id(0) == 0)
    def _():
        out_ref[...] = whole

    @pl.when(pl.program_id(0) > 0)
    def _():
        out_ref[...] += whole


def inverse_factor(gram):
    rows = lax.broadcasted_iota(jnp.int32, (R, LANES), 0)
    lanes = lax.broadcasted_iota(jnp.int32, (R, LANES), 1)
    state = gram + jnp.where(lanes == rows + R, 1.0, 0.0).astype(F32)
    scale = jnp.ones((R, 1), F32)
    for k in range(R):
        pivot = lax.rsqrt(state[k : k + 1, k : k + 1])
        row = state[k : k + 1, :] * pivot
        column = state[:, k : k + 1] * pivot
        below = state - column * row
        state = jnp.where(rows > k, below, jnp.where(rows == k, row, state))
        scale = jnp.where(rows[:, :1] == k, pivot, scale)
    return state[:, R : 2 * R], scale


def head_kernel(t_ref, out_ref):
    columns = out_ref.shape[1]
    inverse, scale = inverse_factor(t_ref[:, columns:])
    out_ref[...] = jnp.dot(
        inverse * scale, t_ref[:, :columns], precision=HIGHEST, preferred_element_type=F32
    )


def last_kernel(t_ref, s_ref, next_ref, basis_ref, coefficients_ref, summed_ref, *, rows_total):
    columns = t_ref.shape[1] - LANES
    inverse, _ = inverse_factor(t_ref[:, columns:])
    basis_ref[...] = (
        jnp.dot(inverse, s_ref[...], precision=HIGHEST, preferred_element_type=F32)
        * math.sqrt(rows_total)
    )
    coefficients = jnp.dot(
        inverse, t_ref[:, :columns], precision=HIGHEST, preferred_element_type=F32
    ) / math.sqrt(rows_total)
    width = N2 * N3
    modes = columns // width
    gram = jnp.zeros((R, R), F32)
    summed = jnp.zeros((R, width), F32)
    pieces = []
    for mode in range(modes):
        part = coefficients[:, mode * width : (mode + 1) * width]
        piece = lax.dot_general(
            next_ref[...], part, (((0,), (1,)), ((), ())), precision=HIGHEST,
            preferred_element_type=F32,
        )
        gram += lax.dot_general(piece, piece, NT, precision=HIGHEST, preferred_element_type=F32)
        summed += jnp.dot(piece, part, precision=HIGHEST, preferred_element_type=F32)
        pieces.append(piece)
    coefficients_ref[...] = jnp.concatenate(pieces, axis=1)
    gram = jnp.concatenate([gram, jnp.zeros((R, LANES - R), F32)], axis=1)
    summed_ref[...] = jnp.concatenate([summed, gram], axis=1)


def second_kernel(summed_ref, pieces_ref, frame_ref, remainder_ref, *, next_rows):
    width = N2 * N3
    inverse, _ = inverse_factor(summed_ref[:, width:])
    frame_ref[...] = jnp.dot(
        inverse, pieces_ref[...], precision=HIGHEST, preferred_element_type=F32
    ) * math.sqrt(next_rows)
    remainder_ref[...] = jnp.dot(
        inverse, summed_ref[:, :width], precision=HIGHEST, preferred_element_type=F32
    ) / math.sqrt(next_rows)


PARAMS = pltpu.CompilerParams(vmem_limit_bytes=32 * 1024 * 1024)


def times_rows(frame, a, block=512):
    rows, columns = a.shape
    return pl.pallas_call(
        rows_kernel,
        grid=(rows // block,),
        in_specs=[
            pl.BlockSpec((R, columns), lambda i: (0, 0)),
            pl.BlockSpec((block, columns), lambda i: (i, 0)),
        ],
        out_specs=pl.BlockSpec((R, block), lambda i: (0, i)),
        out_shape=jax.ShapeDtypeStruct((R, rows), F32),
        compiler_params=PARAMS,
        name="times_rows",
    )(frame, a)


def times_columns(s, a, block=512):
    rows, columns = a.shape
    return pl.pallas_call(
        columns_kernel,
        grid=(rows // block,),
        in_specs=[
            pl.BlockSpec((R, block), lambda i: (0, i)),
            pl.BlockSpec((block, columns), lambda i: (i, 0)),
        ],
        out_specs=pl.BlockSpec((R, columns + LANES), lambda i: (0, 0)),
        out_shape=jax.ShapeDtypeStruct((R, columns + LANES), F32),
        compiler_params=PARAMS,
        name="times_columns",
    )(s, a)


def swap(value, axis, bit):
    size = lax.axis_size(axis)
    return lax.ppermute(value, axis, [(i, i ^ bit) for i in range(size)])


def sum_doubling(value, axis):
    bit = 1
    while bit < lax.axis_size(axis):
        value = value + swap(value, axis, bit)
        bit *= 2
    return value


def sum_halved(value, axis):
    mine = lax.axis_index(axis) % 2
    half = value.shape[1] // 2
    low, high = value[:, :half], value[:, half:]
    kept = jnp.where(mine == 0, low, high) + swap(jnp.where(mine == 0, high, low), axis, 1)
    bit = 2
    while bit < lax.axis_size(axis):
        kept = kept + swap(kept, axis, bit)
        bit *= 2
    other = swap(kept, axis, 1)
    return jnp.concatenate(
        [jnp.where(mine == 0, kept, other), jnp.where(mine == 0, other, kept)], axis=1
    )


def shards(snapshots, sketch, sketch_next):
    rows, columns = snapshots.shape
    rows_total = rows * lax.axis_size("space")
    frame = sketch.T
    for step in range(ITERS + 1):
        s = sum_halved(times_rows(frame, snapshots), "param")
        t = sum_doubling(times_columns(s, snapshots), "space")
        if step < ITERS:
            frame = pl.pallas_call(
                head_kernel,
                out_shape=jax.ShapeDtypeStruct((R, columns), F32),
                compiler_params=PARAMS,
                name="head",
            )(t)
    width = N2 * N3
    local_next = columns // width * R
    basis, pieces, summed = pl.pallas_call(
        lambda *refs: last_kernel(*refs, rows_total=rows_total),
        out_shape=(
            jax.ShapeDtypeStruct((R, rows), F32),
            jax.ShapeDtypeStruct((R, local_next), F32),
            jax.ShapeDtypeStruct((R, width + LANES), F32),
        ),
        compiler_params=PARAMS,
        name="last",
    )(t, s, sketch_next)
    summed = sum_doubling(summed, "param")
    next_rows = local_next * lax.axis_size("param")
    second, remainder = pl.pallas_call(
        lambda *refs: second_kernel(*refs, next_rows=next_rows),
        out_shape=(
            jax.ShapeDtypeStruct((R, local_next), F32),
            jax.ShapeDtypeStruct((R, width), F32),
        ),
        compiler_params=PARAMS,
        name="second",
    )(summed, pieces)
    return basis, second, remainder


def solution(mesh):
    placed = (P("space", "param"), P("param", None), P())
    return jax.shard_map(
        shards,
        mesh=mesh,
        in_specs=placed,
        out_specs=(P(None, "space"), P(None, "param"), P()),
        check_vma=False,
    )
```

```python
import math

import jax
import jax.numpy as jnp
from jax import lax
from jax.experimental import pallas as pl
from jax.experimental.pallas import tpu as pltpu
from jax.sharding import PartitionSpec as P

R = 32
N2 = 16
N3 = 16
ITERS = 3
HIGHEST = lax.Precision.HIGHEST
F32 = jnp.float32
BF16 = jnp.bfloat16
LANES = 128
NT = (((1,), (1,)), ((), ()))


def split(block):
    high = block.astype(BF16)
    return high, (block - high.astype(F32)).astype(BF16)


def stacked(block):
    return jnp.concatenate(split(block), axis=0)


def folded(product):
    turned = product.T
    return turned[:R] + turned[R:]


def rows_kernel(frame_ref, a_ref, out_ref, tall_ref=None):
    block, columns = a_ref.shape
    a = a_ref[...]
    high, low = split(a)
    frame = stacked(frame_ref[...])
    product = lax.dot_general(high, frame, NT, preferred_element_type=F32)
    product += lax.dot_general(low, frame, NT, preferred_element_type=F32)
    out_ref[...] = folded(product)
    if tall_ref is not None:
        at = pl.ds(pl.multiple_of(pl.program_id(0) * block, block), block)
        turned_high, turned_low = split(a.T)
        tall_ref[:columns, at] = turned_high
        tall_ref[columns:, at] = turned_low


def columns_kernel(s_ref, tall_ref, out_ref, sum_ref, *, block):
    columns = tall_ref.shape[0] // 2
    sum_ref[...] = jnp.zeros_like(sum_ref)

    def body(i, carry):
        at = pl.ds(pl.multiple_of(i * block, block), block)
        s = stacked(s_ref[:, at])
        left = jnp.concatenate([tall_ref[:, at], s], axis=0)
        sum_ref[...] += lax.dot_general(left, s, NT, preferred_element_type=F32)
        return carry

    lax.fori_loop(0, s_ref.shape[1] // block, body, 0)
    product = folded(sum_ref[:columns] + sum_ref[columns : 2 * columns])
    both = sum_ref[2 * columns :]
    gram = both[:R] + both[R:]
    gram = gram[:, :R] + gram[:, R:]
    if out_ref.ndim == 2:
        out_ref[:, :columns] = product
        out_ref[:, columns:] = jnp.zeros((R, LANES), F32)
        out_ref[:, columns : columns + R] = gram
    else:
        parts = out_ref.shape[0]
        rows = R // parts
        out_ref[...] = jnp.zeros_like(out_ref)
        for j in range(parts):
            out_ref[j, :R, :] = product[:, j * LANES : (j + 1) * LANES]
            out_ref[j, R : R + rows, :R] = gram[j * rows : (j + 1) * rows]


def unpacked(t_ref):
    if len(t_ref.shape) == 2:
        columns = t_ref.shape[1] - LANES
        return t_ref[:, :columns], t_ref[:, columns:]
    parts = t_ref.shape[0]
    rows = R // parts
    product = jnp.concatenate([t_ref[j, :R, :] for j in range(parts)], axis=1)
    gram = jnp.concatenate([t_ref[j, R : R + rows, :] for j in range(parts)], axis=0)
    return product, gram


def inverse_factor(gram):
    rows = lax.broadcasted_iota(jnp.int32, (R, LANES), 0)
    lanes = lax.broadcasted_iota(jnp.int32, (R, LANES), 1)
    state = gram + jnp.where(lanes == rows + R, 1.0, 0.0).astype(F32)
    scale = jnp.ones((R, 1), F32)
    for k in range(R):
        pivot = lax.rsqrt(state[k : k + 1, k : k + 1])
        row = state[k : k + 1, :] * pivot
        column = state[:, k : k + 1] * pivot
        below = state - column * row
        state = jnp.where(rows > k, below, jnp.where(rows == k, row, state))
        scale = jnp.where(rows[:, :1] == k, pivot, scale)
    return state[:, R : 2 * R], scale


def head_kernel(t_ref, out_ref):
    product, gram = unpacked(t_ref)
    inverse, scale = inverse_factor(gram)
    out_ref[...] = jnp.dot(
        inverse * scale, product, precision=HIGHEST, preferred_element_type=F32
    )


def last_kernel(t_ref, s_ref, next_ref, basis_ref, coefficients_ref, summed_ref, *, rows_total):
    product, gram = unpacked(t_ref)
    columns = product.shape[1]
    inverse, _ = inverse_factor(gram)
    basis_ref[...] = (
        jnp.dot(inverse, s_ref[...], precision=HIGHEST, preferred_element_type=F32)
        * math.sqrt(rows_total)
    )
    coefficients = jnp.dot(
        inverse, product, precision=HIGHEST, preferred_element_type=F32
    ) / math.sqrt(rows_total)
    width = N2 * N3
    modes = columns // width
    gram = jnp.zeros((R, R), F32)
    summed = jnp.zeros((R, width), F32)
    pieces = []
    for mode in range(modes):
        part = coefficients[:, mode * width : (mode + 1) * width]
        piece = lax.dot_general(
            next_ref[...], part, (((0,), (1,)), ((), ())), precision=HIGHEST,
            preferred_element_type=F32,
        )
        gram += lax.dot_general(piece, piece, NT, precision=HIGHEST, preferred_element_type=F32)
        summed += jnp.dot(piece, part, precision=HIGHEST, preferred_element_type=F32)
        pieces.append(piece)
    coefficients_ref[...] = jnp.concatenate(pieces, axis=1)
    gram = jnp.concatenate([gram, jnp.zeros((R, LANES - R), F32)], axis=1)
    summed_ref[...] = jnp.concatenate([summed, gram], axis=1)


def second_kernel(summed_ref, pieces_ref, frame_ref, remainder_ref, *, next_rows):
    width = N2 * N3
    inverse, _ = inverse_factor(summed_ref[:, width:])
    frame_ref[...] = jnp.dot(
        inverse, pieces_ref[...], precision=HIGHEST, preferred_element_type=F32
    ) * math.sqrt(next_rows)
    remainder_ref[...] = jnp.dot(
        inverse, summed_ref[:, :width], precision=HIGHEST, preferred_element_type=F32
    ) / math.sqrt(next_rows)


def params(mebibytes):
    return pltpu.CompilerParams(vmem_limit_bytes=mebibytes * 1024 * 1024)


WHOLE = pl.BlockSpec(memory_space=pltpu.VMEM)


def times_rows(frame, a, keep=False, block=512):
    rows, columns = a.shape
    a = pltpu.with_memory_space_constraint(a, pltpu.HBM)
    out_spec = pl.BlockSpec((R, block), lambda i: (0, i))
    out_shape = jax.ShapeDtypeStruct((R, rows), F32)
    return pl.pallas_call(
        rows_kernel,
        grid=(rows // block,),
        in_specs=[
            pl.BlockSpec((R, columns), lambda i: (0, 0)),
            pl.BlockSpec((block, columns), lambda i: (i, 0)),
        ],
        out_specs=(out_spec, WHOLE) if keep else out_spec,
        out_shape=(out_shape, pltpu.VMEM((2 * columns, rows), BF16)) if keep else out_shape,
        compiler_params=params(24),
        name="times_rows",
    )(frame, a)


def times_columns(s, tall, parts, block=1536):
    columns = tall.shape[0] // 2
    shape = (parts, R + 8, LANES) if parts * LANES == columns else (R, columns + LANES)
    tall = pltpu.with_memory_space_constraint(tall, pltpu.VMEM)
    return pl.pallas_call(
        lambda *refs: columns_kernel(*refs, block=block),
        in_specs=[WHOLE, WHOLE],
        out_specs=WHOLE,
        out_shape=jax.ShapeDtypeStruct(shape, F32),
        scratch_shapes=[pltpu.VMEM((2 * columns + 2 * R, 2 * R), F32)],
        compiler_params=params(8),
        name="times_columns",
    )(s, tall)


def swap(value, axis, bit):
    size = lax.axis_size(axis)
    return lax.ppermute(value, axis, [(i, i ^ bit) for i in range(size)])


def sum_doubling(value, axis):
    bit = 1
    while bit < lax.axis_size(axis):
        value = value + swap(value, axis, bit)
        bit *= 2
    return value


def sum_halved(value, axis):
    mine = lax.axis_index(axis) % 2
    half = value.shape[1] // 2
    low, high = value[:, :half], value[:, half:]
    kept = jnp.where(mine == 0, low, high) + swap(jnp.where(mine == 0, high, low), axis, 1)
    bit = 2
    while bit < lax.axis_size(axis):
        kept = kept + swap(kept, axis, bit)
        bit *= 2
    other = swap(kept, axis, 1)
    return jnp.concatenate(
        [jnp.where(mine == 0, kept, other), jnp.where(mine == 0, other, kept)], axis=1
    )


def sum_parts(value, axis):
    if value.ndim == 2:
        return sum_doubling(value, axis)
    mine = jnp.sum(lax.all_to_all(value, axis, 0, 0, tiled=True), axis=0, keepdims=True)
    return lax.all_to_all(jnp.broadcast_to(mine, value.shape), axis, 0, 0, tiled=True)


def shards(snapshots, sketch, sketch_next):
    rows, columns = snapshots.shape
    rows_total = rows * lax.axis_size("space")
    frame = sketch.T
    s, tall = times_rows(frame, snapshots, keep=True)
    for step in range(ITERS + 1):
        if step:
            s = times_rows(frame, snapshots)
        s = sum_halved(s, "param")
        t = sum_parts(times_columns(s, tall, lax.axis_size("space")), "space")
        if step < ITERS:
            frame = pl.pallas_call(
                head_kernel,
                out_shape=jax.ShapeDtypeStruct((R, columns), F32),
                compiler_params=params(8),
                name="head",
            )(t)
    width = N2 * N3
    local_next = columns // width * R
    basis, pieces, summed = pl.pallas_call(
        lambda *refs: last_kernel(*refs, rows_total=rows_total),
        out_shape=(
            jax.ShapeDtypeStruct((R, rows), F32),
            jax.ShapeDtypeStruct((R, local_next), F32),
            jax.ShapeDtypeStruct((R, width + LANES), F32),
        ),
        compiler_params=params(8),
        name="last",
    )(t, s, sketch_next)
    summed = sum_doubling(summed, "param")
    next_rows = local_next * lax.axis_size("param")
    second, remainder = pl.pallas_call(
        lambda *refs: second_kernel(*refs, next_rows=next_rows),
        out_shape=(
            jax.ShapeDtypeStruct((R, local_next), F32),
            jax.ShapeDtypeStruct((R, width), F32),
        ),
        compiler_params=params(8),
        name="second",
    )(summed, pieces)
    return basis, second, remainder


def solution(mesh):
    placed = (P("space", "param"), P("param", None), P())
    return jax.shard_map(
        shards,
        mesh=mesh,
        in_specs=placed,
        out_specs=(P(None, "space"), P(None, "param"), P()),
        check_vma=False,
    )
```

```python
import math

import jax
import jax.numpy as jnp
from jax import lax
from jax.experimental import pallas as pl
from jax.experimental.pallas import tpu as pltpu
from jax.sharding import PartitionSpec as P

R = 32
N2 = 16
N3 = 16
ITERS = 3
HIGHEST = lax.Precision.HIGHEST
F32 = jnp.float32
BF16 = jnp.bfloat16
LANES = 128
NT = (((1,), (1,)), ((), ()))


def split(block):
    high = block.astype(BF16)
    return high, (block - high.astype(F32)).astype(BF16)


def stacked(block):
    return jnp.concatenate(split(block), axis=0)


def folded(product):
    turned = product.T
    return turned[:R] + turned[R:]


def first_row(keep, piece, rows):
    mine = lax.rem(lax.axis_index("param"), 2)
    half = mine if keep else 1 - mine
    return pl.multiple_of(half * (rows // 2) + piece * (rows // 4), LANES)


def rows_kernel(frame_ref, a_ref, *rest, keep, piece, after):
    out_ref, *rest = rest[after:]
    held, arrived = rest[-2:]
    blocks, block, columns = held.shape
    begin = first_row(keep, piece, a_ref.shape[0])
    copies = [
        pltpu.make_async_copy(
            a_ref.at[pl.ds(begin + i * block, block), :], held.at[i], arrived.at[i]
        )
        for i in range(blocks)
    ]
    for copy in copies:
        copy.start()
    frame = stacked(frame_ref[...])
    for i, copy in enumerate(copies):
        copy.wait()
        a = held[i]
        high, low = split(a)
        product = lax.dot_general(high, frame, NT, preferred_element_type=F32)
        product += lax.dot_general(low, frame, NT, preferred_element_type=F32)
        at = slice(i * block, (i + 1) * block)
        out_ref[:, at] = folded(product)
        if len(rest) > 2:
            turned_high, turned_low = split(a.T)
            rest[0][:columns, at] = turned_high
            rest[0][columns:, at] = turned_low


def columns_kernel(*refs, terms, begin, end):
    sources, rest = refs[: 2 * terms], list(refs[2 * terms :])
    total = None if begin else rest.pop(0)[...]
    for i in range(terms):
        s = stacked(sources[2 * i][...])
        left = jnp.concatenate([sources[2 * i + 1][...], s], axis=0)
        term = lax.dot_general(left, s, NT, preferred_element_type=F32)
        total = term if total is None else total + term
    if not end:
        rest[0][...] = total
        return
    left_ref, right_ref = rest
    half = right_ref.shape[1]
    columns = 2 * half
    product = folded(total[:columns] + total[columns : 2 * columns])
    both = total[2 * columns :]
    gram = both[:R] + both[R:]
    gram = gram[:, :R] + gram[:, R:]
    left_ref[:, :half] = product[:, :half]
    left_ref[:, half:] = jnp.zeros((R, LANES), F32)
    left_ref[:, half : half + R] = gram
    right_ref[...] = product[:, half:]


def unpacked(left_ref, right_ref):
    half = right_ref.shape[1]
    product = jnp.concatenate([left_ref[:, :half], right_ref[...]], axis=1)
    return product, left_ref[:, half:]


def inverse_factor(gram):
    rows = lax.broadcasted_iota(jnp.int32, (R, LANES), 0)
    lanes = lax.broadcasted_iota(jnp.int32, (R, LANES), 1)
    state = gram + jnp.where(lanes == rows + R, 1.0, 0.0).astype(F32)
    scale = jnp.ones((R, 1), F32)
    for k in range(R):
        pivot = lax.rsqrt(state[k : k + 1, k : k + 1])
        row = state[k : k + 1, :] * pivot
        column = state[:, k : k + 1] * pivot
        below = state - column * row
        state = jnp.where(rows > k, below, jnp.where(rows == k, row, state))
        scale = jnp.where(rows[:, :1] == k, pivot, scale)
    return state[:, R : 2 * R], scale


def head_kernel(left_ref, right_ref, out_ref):
    product, gram = unpacked(left_ref, right_ref)
    inverse, scale = inverse_factor(gram)
    out_ref[...] = jnp.dot(
        inverse * scale, product, precision=HIGHEST, preferred_element_type=F32
    )


def last_kernel(left_ref, right_ref, *refs, rows_total, roles):
    s_refs, (next_ref, basis_ref, coefficients_ref, summed_ref) = refs[:-4], refs[-4:]
    product, gram = unpacked(left_ref, right_ref)
    columns = product.shape[1]
    inverse, _ = inverse_factor(gram)
    for s_ref, (keep, piece) in zip(s_refs, roles):
        begin = first_row(keep, piece, basis_ref.shape[1])
        basis_ref[:, pl.ds(begin, s_ref.shape[1])] = jnp.dot(
            inverse, s_ref[...], precision=HIGHEST, preferred_element_type=F32
        ) * math.sqrt(rows_total)
    coefficients = jnp.dot(
        inverse, product, precision=HIGHEST, preferred_element_type=F32
    ) / math.sqrt(rows_total)
    width = N2 * N3
    modes = columns // width
    gram = jnp.zeros((R, R), F32)
    summed = jnp.zeros((R, width), F32)
    pieces = []
    for mode in range(modes):
        part = coefficients[:, mode * width : (mode + 1) * width]
        piece = lax.dot_general(
            next_ref[...], part, (((0,), (1,)), ((), ())), precision=HIGHEST,
            preferred_element_type=F32,
        )
        gram += lax.dot_general(piece, piece, NT, precision=HIGHEST, preferred_element_type=F32)
        summed += jnp.dot(piece, part, precision=HIGHEST, preferred_element_type=F32)
        pieces.append(piece)
    coefficients_ref[...] = jnp.concatenate(pieces, axis=1)
    gram = jnp.concatenate([gram, jnp.zeros((R, LANES - R), F32)], axis=1)
    summed_ref[...] = jnp.concatenate([summed, gram], axis=1)


def second_kernel(summed_ref, pieces_ref, frame_ref, remainder_ref, *, next_rows):
    width = N2 * N3
    inverse, _ = inverse_factor(summed_ref[:, width:])
    frame_ref[...] = jnp.dot(
        inverse, pieces_ref[...], precision=HIGHEST, preferred_element_type=F32
    ) * math.sqrt(next_rows)
    remainder_ref[...] = jnp.dot(
        inverse, summed_ref[:, :width], precision=HIGHEST, preferred_element_type=F32
    ) / math.sqrt(next_rows)


def params(mebibytes):
    return pltpu.CompilerParams(vmem_limit_bytes=mebibytes * 1024 * 1024)


WHOLE = pl.BlockSpec(memory_space=pltpu.VMEM)
ANYWHERE = pl.BlockSpec(memory_space=pl.ANY)


ROLES = ((False, 0), (True, 0), (False, 1), (True, 1))


def times_rows(frame, a, role, first, after=(), block=256):
    rows, columns = a.shape
    part = rows // 4
    a = pltpu.with_memory_space_constraint(a, pltpu.HBM)
    out_shape = [pltpu.VMEM((R, part), F32)]
    if first:
        out_shape.append(pltpu.VMEM((2 * columns, part), BF16))
    keep, piece = role
    return pl.pallas_call(
        lambda *refs: rows_kernel(*refs, keep=keep, piece=piece, after=len(after)),
        in_specs=[WHOLE, pl.BlockSpec(memory_space=pltpu.HBM)] + [ANYWHERE] * len(after),
        out_specs=[WHOLE] * len(out_shape),
        out_shape=out_shape,
        scratch_shapes=[
            pltpu.VMEM((part // block, block, columns), F32),
            pltpu.SemaphoreType.DMA((part // block,)),
        ],
        compiler_params=params(12),
        cost_estimate=pl.CostEstimate(
            flops=8 * R * part * columns, bytes_accessed=4 * part * columns, transcendentals=0
        ),
        name="times_rows",
    )(frame, a, *after)


def add_after(left, right, after):
    def kernel(left_ref, right_ref, after_ref, out_ref):
        out_ref[...] = left_ref[...] + right_ref[...]

    return pl.pallas_call(
        kernel,
        in_specs=[WHOLE, WHOLE, ANYWHERE],
        out_specs=WHOLE,
        out_shape=pltpu.VMEM(left.shape, left.dtype),
        compiler_params=params(4),
        name="add_after",
    )(left, right, after)


def times_columns(total, pairs, end):
    columns, part = pairs[0][1].shape
    operands = [
        x
        for s, tall in pairs
        for x in (s, pltpu.with_memory_space_constraint(tall, pltpu.VMEM))
    ]
    if total is not None:
        operands.append(total)
    if end:
        out_shape = (
            jax.ShapeDtypeStruct((R, columns // 4 + LANES), F32),
            jax.ShapeDtypeStruct((R, columns // 4), F32),
        )
    else:
        out_shape = pltpu.VMEM((columns + 2 * R, 2 * R), F32)
    return pl.pallas_call(
        lambda *refs: columns_kernel(*refs, terms=len(pairs), begin=total is None, end=end),
        in_specs=[WHOLE] * len(operands),
        out_specs=(WHOLE, WHOLE) if end else WHOLE,
        out_shape=out_shape,
        compiler_params=params(8),
        cost_estimate=pl.CostEstimate(
            flops=4 * R * part * columns * len(pairs),
            bytes_accessed=2 * part * columns * len(pairs),
            transcendentals=0,
        ),
        name="times_columns",
    )(*operands)


def swap(value, axis, bit):
    size = lax.axis_size(axis)
    return lax.ppermute(value, axis, [(i, i ^ bit) for i in range(size)])


def sum_doubling(value, axis):
    bit = 1
    while bit < lax.axis_size(axis):
        value = value + swap(value, axis, bit)
        bit *= 2
    return value


def sum_both(left, right, axis):
    bits = []
    while 2 ** len(bits) < lax.axis_size(axis):
        bits.append(2 ** len(bits))
    for i in range(len(bits)):
        left_other = swap(left, axis, bits[i])
        right_other = swap(right, axis, bits[i - 1])
        left = left + left_other
        right = right + right_other
    return left, right


def sum_rest(value, axis, after):
    bit = 2
    while bit < lax.axis_size(axis):
        value = add_after(value, swap(value, axis, bit), after)
        bit *= 2
    return value


def shards(snapshots, sketch, sketch_next):
    rows, columns = snapshots.shape
    rows_total = rows * lax.axis_size("space")
    frame = sketch.T
    talls = []
    for step in range(ITERS + 1):
        first = step == 0

        def role_rows(keep, piece, after=()):
            s, *tall = times_rows(frame, snapshots, (keep, piece), first, after)
            talls.extend(tall)
            return s

        sent = role_rows(False, 0)
        kept = role_rows(True, 0, [sent])
        start = kept + swap(sent, "param", 1)
        sent = role_rows(False, 1, [start])
        kept = role_rows(True, 1, [sent])
        near = kept + swap(sent, "param", 1)
        start = sum_rest(start, "param", kept)
        full = [swap(start, "param", 1), start]
        total = times_columns(None, [(full[1], talls[1]), (full[0], talls[0])], False)
        near = sum_rest(near, "param", total)
        full += [swap(near, "param", 1), near]
        total = times_columns(total, [(full[3], talls[3])], False)
        left, right = times_columns(total, [(full[2], talls[2])], True)
        left, right = sum_both(left, right, "space")
        if step < ITERS:
            frame = pl.pallas_call(
                head_kernel,
                out_shape=jax.ShapeDtypeStruct((R, columns), F32),
                compiler_params=params(8),
                name="head",
            )(left, right)
    width = N2 * N3
    local_next = columns // width * R
    basis, pieces, summed = pl.pallas_call(
        lambda *refs: last_kernel(*refs, rows_total=rows_total, roles=ROLES),
        out_shape=(
            jax.ShapeDtypeStruct((R, rows), F32),
            jax.ShapeDtypeStruct((R, local_next), F32),
            jax.ShapeDtypeStruct((R, width + LANES), F32),
        ),
        compiler_params=params(8),
        name="last",
    )(left, right, *full, sketch_next)
    summed = sum_doubling(summed, "param")
    next_rows = local_next * lax.axis_size("param")
    second, remainder = pl.pallas_call(
        lambda *refs: second_kernel(*refs, next_rows=next_rows),
        out_shape=(
            jax.ShapeDtypeStruct((R, local_next), F32),
            jax.ShapeDtypeStruct((R, width), F32),
        ),
        compiler_params=params(8),
        name="second",
    )(summed, pieces)
    return basis, second, remainder


def solution(mesh):
    placed = (P("space", "param"), P("param", None), P())
    return jax.shard_map(
        shards,
        mesh=mesh,
        in_specs=placed,
        out_specs=(P(None, "space"), P(None, "param"), P()),
        check_vma=False,
    )
```

```python
import math

import jax
import jax.numpy as jnp
from jax import lax
from jax.experimental import pallas as pl
from jax.experimental.pallas import tpu as pltpu
from jax.sharding import PartitionSpec as P

R = 32
N2 = 16
N3 = 16
ITERS = 3
HIGHEST = lax.Precision.HIGHEST
F32 = jnp.float32
BF16 = jnp.bfloat16
LANES = 128
NT = (((1,), (1,)), ((), ()))


def split(block):
    high = block.astype(BF16)
    return high, (block - high.astype(F32)).astype(BF16)


def stacked(block):
    return jnp.concatenate(split(block), axis=0)


def folded(product):
    turned = product.T
    return turned[:R] + turned[R:]


def first_row(keep, piece, rows):
    mine = lax.rem(lax.axis_index("param"), 2)
    half = mine if keep else 1 - mine
    return pl.multiple_of(half * (rows // 2) + piece * (rows // 4), LANES)


def keep_rows(a_ref, wide_ref, tall_ref, held, arrived, keep, piece):
    slots, block, columns = held.shape
    part = tall_ref.shape[1]
    begin = first_row(keep, piece, a_ref.shape[0])
    copies = [
        pltpu.make_async_copy(
            a_ref.at[pl.ds(begin + i * block, block), :],
            held.at[i % slots],
            arrived.at[i % slots],
        )
        for i in range(part // block)
    ]
    for copy in copies[:slots]:
        copy.start()
    for i, copy in enumerate(copies):
        copy.wait()
        a = held[i % slots]
        wide_ref[i * block : (i + 1) * block, :], wide_ref[part + i * block : part + (i + 1) * block, :] = split(a)
        tall_ref[:columns, i * block : (i + 1) * block], tall_ref[columns:, i * block : (i + 1) * block] = split(a.T)
        if i + slots < len(copies):
            copies[i + slots].start()


def rows_product(frame, wide_ref, out_ref):
    part = out_ref.shape[1]
    product = lax.dot_general(wide_ref[...], frame, NT, preferred_element_type=F32)
    out_ref[...] = folded(product[:part] + product[part:])


def first_kernel(frame_ref, a_ref, *rest, keep, piece, after):
    out_ref, wide_ref, tall_ref, held, arrived = rest[after:]
    keep_rows(a_ref, wide_ref, tall_ref, held, arrived, keep, piece)
    rows_product(stacked(frame_ref[...]), wide_ref, out_ref)


def lead_kernel(inverse_ref, left_ref, right_ref, wide_ref, out_ref, frame_ref):
    product, _ = unpacked(left_ref, right_ref)
    frame_ref[...] = stacked(
        jnp.dot(inverse_ref[...], product, precision=HIGHEST, preferred_element_type=F32)
    )
    rows_product(frame_ref[...], wide_ref, out_ref)


def rows_kernel(frame_ref, wide_ref, after_ref, out_ref):
    rows_product(frame_ref[...], wide_ref, out_ref)


def columns_kernel(*refs, terms, begin, end):
    sources, rest = refs[: 2 * terms], list(refs[2 * terms :])
    total = None if begin else rest.pop(0)[...]
    for i in range(terms):
        s = stacked(sources[2 * i][...])
        left = jnp.concatenate([sources[2 * i + 1][...], s], axis=0)
        term = lax.dot_general(left, s, NT, preferred_element_type=F32)
        total = term if total is None else total + term
    if not end:
        rest[0][...] = total
        return
    left_ref, right_ref = rest
    half = right_ref.shape[1]
    columns = 2 * half
    product = folded(total[:columns] + total[columns : 2 * columns])
    both = total[2 * columns :]
    gram = both[:R] + both[R:]
    gram = gram[:, :R] + gram[:, R:]
    left_ref[:, :half] = product[:, :half]
    left_ref[:, half:] = jnp.zeros((R, LANES), F32)
    left_ref[:, half : half + R] = gram
    right_ref[...] = product[:, half:]


def unpacked(left_ref, right_ref):
    half = right_ref.shape[1]
    product = jnp.concatenate([left_ref[:, :half], right_ref[...]], axis=1)
    return product, left_ref[:, half:]


def inverse_factor(gram):
    rows = lax.broadcasted_iota(jnp.int32, (R, LANES), 0)
    lanes = lax.broadcasted_iota(jnp.int32, (R, LANES), 1)
    state = gram + jnp.where(lanes == rows + R, 1.0, 0.0).astype(F32)
    scale = jnp.ones((R, 1), F32)
    for k in range(R):
        pivot = lax.rsqrt(state[k : k + 1, k : k + 1])
        row = state[k : k + 1, :] * pivot
        column = state[:, k : k + 1] * pivot
        below = state - column * row
        state = jnp.where(rows > k, below, jnp.where(rows == k, row, state))
        scale = jnp.where(rows[:, :1] == k, pivot, scale)
    return state[:, R : 2 * R], scale


def factor_kernel(left_ref, out_ref, *, scaled):
    inverse, scale = inverse_factor(left_ref[:, left_ref.shape[1] - LANES :])
    out_ref[...] = inverse * scale if scaled else inverse


def last_kernel(inverse_ref, left_ref, right_ref, *refs, rows_total, roles):
    s_refs, (next_ref, basis_ref, coefficients_ref, summed_ref) = refs[:-4], refs[-4:]
    product, _ = unpacked(left_ref, right_ref)
    columns = product.shape[1]
    inverse = inverse_ref[...]
    for s_ref, (keep, piece) in zip(s_refs, roles):
        begin = first_row(keep, piece, basis_ref.shape[1])
        basis_ref[:, pl.ds(begin, s_ref.shape[1])] = jnp.dot(
            inverse, s_ref[...], precision=HIGHEST, preferred_element_type=F32
        ) * math.sqrt(rows_total)
    coefficients = jnp.dot(
        inverse, product, precision=HIGHEST, preferred_element_type=F32
    ) / math.sqrt(rows_total)
    width = N2 * N3
    modes = columns // width
    gram = jnp.zeros((R, R), F32)
    summed = jnp.zeros((R, width), F32)
    pieces = []
    for mode in range(modes):
        part = coefficients[:, mode * width : (mode + 1) * width]
        piece = lax.dot_general(
            next_ref[...], part, (((0,), (1,)), ((), ())), precision=HIGHEST,
            preferred_element_type=F32,
        )
        gram += lax.dot_general(piece, piece, NT, precision=HIGHEST, preferred_element_type=F32)
        summed += jnp.dot(piece, part, precision=HIGHEST, preferred_element_type=F32)
        pieces.append(piece)
    coefficients_ref[...] = jnp.concatenate(pieces, axis=1)
    gram = jnp.concatenate([gram, jnp.zeros((R, LANES - R), F32)], axis=1)
    summed_ref[...] = jnp.concatenate([summed, gram], axis=1)


def second_kernel(summed_ref, pieces_ref, frame_ref, remainder_ref, *, next_rows):
    width = N2 * N3
    inverse, _ = inverse_factor(summed_ref[:, width:])
    frame_ref[...] = jnp.dot(
        inverse, pieces_ref[...], precision=HIGHEST, preferred_element_type=F32
    ) * math.sqrt(next_rows)
    remainder_ref[...] = jnp.dot(
        inverse, summed_ref[:, :width], precision=HIGHEST, preferred_element_type=F32
    ) / math.sqrt(next_rows)


def params(mebibytes):
    return pltpu.CompilerParams(vmem_limit_bytes=mebibytes * 1024 * 1024)


WHOLE = pl.BlockSpec(memory_space=pltpu.VMEM)
ANYWHERE = pl.BlockSpec(memory_space=pl.ANY)


ROLES = ((False, 0), (True, 0), (False, 1), (True, 1))


def rows_cost(part, columns):
    return pl.CostEstimate(
        flops=8 * R * part * columns, bytes_accessed=4 * part * columns, transcendentals=0
    )


def first_rows(frame, a, role, after, block=256, slots=4):
    rows, columns = a.shape
    part = rows // 4
    a = pltpu.with_memory_space_constraint(a, pltpu.HBM)
    keep, piece = role
    return pl.pallas_call(
        lambda *refs: first_kernel(*refs, keep=keep, piece=piece, after=len(after)),
        in_specs=[WHOLE, pl.BlockSpec(memory_space=pltpu.HBM)] + [ANYWHERE] * len(after),
        out_specs=[WHOLE] * 3,
        out_shape=(
            pltpu.VMEM((R, part), F32),
            pltpu.VMEM((2 * part, columns), BF16),
            pltpu.VMEM((2 * columns, part), BF16),
        ),
        scratch_shapes=[
            pltpu.VMEM((slots, block, columns), F32),
            pltpu.SemaphoreType.DMA((slots,)),
        ],
        compiler_params=params(10),
        cost_estimate=rows_cost(part, columns),
        name="first_rows",
    )(frame, a, *after)


def lead_rows(inverse, left, right, wide):
    part, columns = wide.shape[0] // 2, wide.shape[1]
    return pl.pallas_call(
        lead_kernel,
        in_specs=[WHOLE] * 4,
        out_specs=[WHOLE] * 2,
        out_shape=(pltpu.VMEM((R, part), F32), pltpu.VMEM((2 * R, columns), BF16)),
        compiler_params=params(6),
        cost_estimate=rows_cost(part, columns),
        name="lead_rows",
    )(inverse, left, right, pltpu.with_memory_space_constraint(wide, pltpu.VMEM))


def times_rows(frame, wide, after):
    part, columns = wide.shape[0] // 2, wide.shape[1]
    return pl.pallas_call(
        rows_kernel,
        in_specs=[WHOLE, WHOLE, ANYWHERE],
        out_specs=WHOLE,
        out_shape=pltpu.VMEM((R, part), F32),
        compiler_params=params(6),
        cost_estimate=rows_cost(part, columns),
        name="times_rows",
    )(frame, pltpu.with_memory_space_constraint(wide, pltpu.VMEM), after)


def add_after(left, right, after):
    def kernel(left_ref, right_ref, after_ref, out_ref):
        out_ref[...] = left_ref[...] + right_ref[...]

    return pl.pallas_call(
        kernel,
        in_specs=[WHOLE, WHOLE, ANYWHERE],
        out_specs=WHOLE,
        out_shape=pltpu.VMEM(left.shape, left.dtype),
        compiler_params=params(4),
        name="add_after",
    )(left, right, after)


def times_columns(total, pairs, end):
    columns, part = pairs[0][1].shape
    operands = [
        x
        for s, tall in pairs
        for x in (s, pltpu.with_memory_space_constraint(tall, pltpu.VMEM))
    ]
    if total is not None:
        operands.append(total)
    if end:
        out_shape = (
            jax.ShapeDtypeStruct((R, columns // 4 + LANES), F32),
            jax.ShapeDtypeStruct((R, columns // 4), F32),
        )
    else:
        out_shape = pltpu.VMEM((columns + 2 * R, 2 * R), F32)
    return pl.pallas_call(
        lambda *refs: columns_kernel(*refs, terms=len(pairs), begin=total is None, end=end),
        in_specs=[WHOLE] * len(operands),
        out_specs=(WHOLE, WHOLE) if end else WHOLE,
        out_shape=out_shape,
        compiler_params=params(8),
        cost_estimate=pl.CostEstimate(
            flops=4 * R * part * columns * len(pairs),
            bytes_accessed=2 * part * columns * len(pairs),
            transcendentals=0,
        ),
        name="times_columns",
    )(*operands)


def swap(value, axis, bit):
    size = lax.axis_size(axis)
    return lax.ppermute(value, axis, [(i, i ^ bit) for i in range(size)])


def sum_doubling(value, axis):
    bit = 1
    while bit < lax.axis_size(axis):
        value = value + swap(value, axis, bit)
        bit *= 2
    return value


def sum_both(left, right, axis, scaled):
    bits = []
    while 2 ** len(bits) < lax.axis_size(axis):
        bits.append(2 ** len(bits))
    for i in range(len(bits)):
        left_other = swap(left, axis, bits[i])
        right_other = swap(right, axis, bits[i - 1])
        left = left + left_other
        if i < len(bits) - 1:
            right = right + right_other
    inverse = pl.pallas_call(
        lambda *refs: factor_kernel(*refs, scaled=scaled),
        out_shape=jax.ShapeDtypeStruct((R, R), F32),
        compiler_params=params(4),
        name="factor",
    )(left)
    return inverse, left, add_after(right, right_other, inverse)


def sum_rest(value, axis, after):
    bit = 2
    while bit < lax.axis_size(axis):
        value = add_after(value, swap(value, axis, bit), after)
        bit *= 2
    return value


def shards(snapshots, sketch, sketch_next):
    rows = snapshots.shape[0]
    columns = snapshots.shape[1]
    rows_total = rows * lax.axis_size("space")
    kept_rows = {}

    for step in range(ITERS + 1):

        def role_rows(role, *after):
            if step:
                return times_rows(frame, kept_rows[role][0], after[0])
            s, *kept_rows[role] = first_rows(sketch.T, snapshots, role, after)
            return s

        if step:
            sent, frame = lead_rows(inverse, left, right, kept_rows[False, 0][0])
        else:
            sent = role_rows((False, 0))
        kept = role_rows((True, 0), sent)
        start = kept + swap(sent, "param", 1)
        sent = role_rows((False, 1), start)
        kept = role_rows((True, 1), sent)
        near = kept + swap(sent, "param", 1)
        start = sum_rest(start, "param", kept)
        full = [swap(start, "param", 1), start]
        talls = [kept_rows[role][1] for role in ROLES]
        total = times_columns(None, [(full[1], talls[1]), (full[0], talls[0])], False)
        near = sum_rest(near, "param", total)
        full += [swap(near, "param", 1), near]
        total = times_columns(total, [(full[3], talls[3])], False)
        left, right = times_columns(total, [(full[2], talls[2])], True)
        inverse, left, right = sum_both(left, right, "space", step < ITERS)
    width = N2 * N3
    local_next = columns // width * R
    basis, pieces, summed = pl.pallas_call(
        lambda *refs: last_kernel(*refs, rows_total=rows_total, roles=ROLES),
        out_shape=(
            jax.ShapeDtypeStruct((R, rows), F32),
            jax.ShapeDtypeStruct((R, local_next), F32),
            jax.ShapeDtypeStruct((R, width + LANES), F32),
        ),
        compiler_params=params(8),
        name="last",
    )(inverse, left, right, *full, sketch_next)
    summed = sum_doubling(summed, "param")
    next_rows = local_next * lax.axis_size("param")
    second, remainder = pl.pallas_call(
        lambda *refs: second_kernel(*refs, next_rows=next_rows),
        out_shape=(
            jax.ShapeDtypeStruct((R, local_next), F32),
            jax.ShapeDtypeStruct((R, width), F32),
        ),
        compiler_params=params(8),
        name="second",
    )(summed, pieces)
    return basis, second, remainder


def solution(mesh):
    placed = (P("space", "param"), P("param", None), P())
    return jax.shard_map(
        shards,
        mesh=mesh,
        in_specs=placed,
        out_specs=(P(None, "space"), P(None, "param"), P()),
        check_vma=False,
    )
```

```python
import math

import jax
import jax.numpy as jnp
from jax import lax
from jax.experimental import pallas as pl
from jax.experimental.pallas import tpu as pltpu
from jax.sharding import PartitionSpec as P

R = 32
N2 = 16
N3 = 16
ITERS = 3
HIGHEST = lax.Precision.HIGHEST
F32 = jnp.float32
BF16 = jnp.bfloat16
LANES = 128
NT = (((1,), (1,)), ((), ()))


def split(block):
    high = block.astype(BF16)
    return high, (block - high.astype(F32)).astype(BF16)


def stacked(block):
    return jnp.concatenate(split(block), axis=0)


def folded(product):
    turned = product.T
    return turned[:R] + turned[R:]


def first_row(keep, piece, rows):
    mine = lax.rem(lax.axis_index("param"), 2)
    half = mine if keep else 1 - mine
    return pl.multiple_of(half * (rows // 2) + piece * (rows // 4), LANES)


def keep_rows(a_ref, wide_ref, tall_ref, held, arrived, keep, piece, stored=None):
    slots, block, columns = held.shape
    part = tall_ref.shape[1]
    begin = first_row(keep, piece, a_ref.shape[0])
    copies = [
        pltpu.make_async_copy(
            a_ref.at[pl.ds(begin + i * block, block), :],
            held.at[i % slots],
            arrived.at[i % slots],
        )
        for i in range(part // block)
    ]
    leaving = []
    for copy in copies[:slots]:
        copy.start()
    for i, copy in enumerate(copies):
        copy.wait()
        at = i * block
        for half, value in enumerate(split(held[i % slots])):
            rows = slice(half * part + at, half * part + at + block)
            wide_ref[rows, :] = value
            tall_ref[half * columns : (half + 1) * columns, at : at + block] = value.T
            if stored is not None:
                leaving.append(
                    pltpu.make_async_copy(
                        wide_ref.at[rows, :], stored[0].at[rows, :], stored[1].at[2 * i + half]
                    )
                )
                leaving[-1].start()
        if i + slots < len(copies):
            copies[i + slots].start()
    return leaving


def rows_product(frame, wide_ref, out_ref):
    part = out_ref.shape[1]
    product = lax.dot_general(wide_ref[...], frame, NT, preferred_element_type=F32)
    out_ref[...] = folded(product[:part] + product[part:])


def first_kernel(frame_ref, a_ref, *rest, keep, piece, after):
    out_ref, stored_ref, tall_ref, held, arrived, *rest = rest[after:]
    wide_ref, *sent = rest or [stored_ref]
    stored = (stored_ref, *sent) if sent else None
    leaving = keep_rows(a_ref, wide_ref, tall_ref, held, arrived, keep, piece, stored)
    rows_product(stacked(frame_ref[...]), wide_ref, out_ref)
    for copy in leaving:
        copy.wait()


def lead_kernel(inverse_ref, left_ref, right_ref, wide_ref, out_ref, frame_ref):
    product, _ = unpacked(left_ref, right_ref)
    frame_ref[...] = stacked(
        jnp.dot(inverse_ref[...], product, precision=HIGHEST, preferred_element_type=F32)
    )
    rows_product(frame_ref[...], wide_ref, out_ref)


def rows_kernel(frame_ref, wide_ref, after_ref, out_ref):
    rows_product(frame_ref[...], wide_ref, out_ref)


def columns_kernel(*refs, terms, begin, end):
    sources, rest = refs[: 2 * terms], list(refs[2 * terms :])
    total = None if begin else rest.pop(0)[...]
    for i in range(terms):
        s = stacked(sources[2 * i][...])
        left = jnp.concatenate([sources[2 * i + 1][...], s], axis=0)
        term = lax.dot_general(left, s, NT, preferred_element_type=F32)
        total = term if total is None else total + term
    if not end:
        rest[0][...] = total
        return
    left_ref, right_ref = rest
    half = right_ref.shape[1]
    columns = 2 * half
    product = folded(total[:columns] + total[columns : 2 * columns])
    both = total[2 * columns :]
    gram = both[:R] + both[R:]
    gram = gram[:, :R] + gram[:, R:]
    left_ref[:, :half] = product[:, :half]
    left_ref[:, half:] = jnp.zeros((R, LANES), F32)
    left_ref[:, half : half + R] = gram
    right_ref[...] = product[:, half:]


def unpacked(left_ref, right_ref):
    half = right_ref.shape[1]
    product = jnp.concatenate([left_ref[:, :half], right_ref[...]], axis=1)
    return product, left_ref[:, half:]


def inverse_factor(gram):
    rows = lax.broadcasted_iota(jnp.int32, (R, LANES), 0)
    lanes = lax.broadcasted_iota(jnp.int32, (R, LANES), 1)
    state = gram + jnp.where(lanes == rows + R, 1.0, 0.0).astype(F32)
    scale = jnp.ones((R, 1), F32)
    for k in range(R):
        pivot = lax.rsqrt(state[k : k + 1, k : k + 1])
        row = state[k : k + 1, :] * pivot
        column = state[:, k : k + 1] * pivot
        below = state - column * row
        state = jnp.where(rows > k, below, jnp.where(rows == k, row, state))
        scale = jnp.where(rows[:, :1] == k, pivot, scale)
    return state[:, R : 2 * R], scale


def factor_kernel(left_ref, out_ref, *, scaled):
    inverse, scale = inverse_factor(left_ref[:, left_ref.shape[1] - LANES :])
    out_ref[...] = inverse * scale if scaled else inverse


def last_kernel(inverse_ref, left_ref, right_ref, *refs, rows_total, roles):
    s_refs, (next_ref, basis_ref, coefficients_ref, summed_ref) = refs[:-4], refs[-4:]
    product, _ = unpacked(left_ref, right_ref)
    columns = product.shape[1]
    inverse = inverse_ref[...]
    for s_ref, (keep, piece) in zip(s_refs, roles):
        begin = first_row(keep, piece, basis_ref.shape[1])
        basis_ref[:, pl.ds(begin, s_ref.shape[1])] = jnp.dot(
            inverse, s_ref[...], precision=HIGHEST, preferred_element_type=F32
        ) * math.sqrt(rows_total)
    coefficients = jnp.dot(
        inverse, product, precision=HIGHEST, preferred_element_type=F32
    ) / math.sqrt(rows_total)
    width = N2 * N3
    modes = columns // width
    gram = jnp.zeros((R, R), F32)
    summed = jnp.zeros((R, width), F32)
    pieces = []
    for mode in range(modes):
        part = coefficients[:, mode * width : (mode + 1) * width]
        piece = lax.dot_general(
            next_ref[...], part, (((0,), (1,)), ((), ())), precision=HIGHEST,
            preferred_element_type=F32,
        )
        gram += lax.dot_general(piece, piece, NT, precision=HIGHEST, preferred_element_type=F32)
        summed += jnp.dot(piece, part, precision=HIGHEST, preferred_element_type=F32)
        pieces.append(piece)
    coefficients_ref[...] = jnp.concatenate(pieces, axis=1)
    gram = jnp.concatenate([gram, jnp.zeros((R, LANES - R), F32)], axis=1)
    summed_ref[...] = jnp.concatenate([summed, gram], axis=1)


def second_kernel(summed_ref, pieces_ref, frame_ref, remainder_ref, *, next_rows):
    width = N2 * N3
    inverse, _ = inverse_factor(summed_ref[:, width:])
    frame_ref[...] = jnp.dot(
        inverse, pieces_ref[...], precision=HIGHEST, preferred_element_type=F32
    ) * math.sqrt(next_rows)
    remainder_ref[...] = jnp.dot(
        inverse, summed_ref[:, :width], precision=HIGHEST, preferred_element_type=F32
    ) / math.sqrt(next_rows)


def params(mebibytes):
    return pltpu.CompilerParams(vmem_limit_bytes=mebibytes * 1024 * 1024)


WHOLE = pl.BlockSpec(memory_space=pltpu.VMEM)
ANYWHERE = pl.BlockSpec(memory_space=pl.ANY)


ROLES = ((False, 0), (True, 0), (False, 1), (True, 1))


def rows_cost(part, columns):
    return pl.CostEstimate(
        flops=8 * R * part * columns, bytes_accessed=4 * part * columns, transcendentals=0
    )


def first_rows(frame, a, role, after, block=256, slots=4):
    rows, columns = a.shape
    part = rows // 4
    a = pltpu.with_memory_space_constraint(a, pltpu.HBM)
    keep, piece = role
    wide = (2 * part, columns)
    scratch = [pltpu.VMEM((slots, block, columns), F32), pltpu.SemaphoreType.DMA((slots,))]
    if piece:
        scratch += [pltpu.VMEM(wide, BF16), pltpu.SemaphoreType.DMA((2 * (part // block),))]
    return pl.pallas_call(
        lambda *refs: first_kernel(*refs, keep=keep, piece=piece, after=len(after)),
        in_specs=[WHOLE, pl.BlockSpec(memory_space=pltpu.HBM)] + [ANYWHERE] * len(after),
        out_specs=[WHOLE, pl.BlockSpec(memory_space=pltpu.HBM) if piece else WHOLE, WHOLE],
        out_shape=(
            pltpu.VMEM((R, part), F32),
            pltpu.HBM(wide, BF16) if piece else pltpu.VMEM(wide, BF16),
            pltpu.VMEM((2 * columns, part), BF16),
        ),
        scratch_shapes=scratch,
        compiler_params=params(16 if piece else 10),
        cost_estimate=rows_cost(part, columns),
        name="first_rows",
    )(frame, a, *after)


def lead_rows(inverse, left, right, wide):
    part, columns = wide.shape[0] // 2, wide.shape[1]
    return pl.pallas_call(
        lead_kernel,
        in_specs=[WHOLE] * 4,
        out_specs=[WHOLE] * 2,
        out_shape=(pltpu.VMEM((R, part), F32), pltpu.VMEM((2 * R, columns), BF16)),
        compiler_params=params(12),
        cost_estimate=rows_cost(part, columns),
        name="lead_rows",
    )(inverse, left, right, pltpu.with_memory_space_constraint(wide, pltpu.VMEM))


def times_rows(frame, wide, after):
    part, columns = wide.shape[0] // 2, wide.shape[1]
    return pl.pallas_call(
        rows_kernel,
        in_specs=[WHOLE, WHOLE, ANYWHERE],
        out_specs=WHOLE,
        out_shape=pltpu.VMEM((R, part), F32),
        compiler_params=params(12),
        cost_estimate=rows_cost(part, columns),
        name="times_rows",
    )(frame, pltpu.with_memory_space_constraint(wide, pltpu.VMEM), after)


def add_after(left, right, after):
    def kernel(left_ref, right_ref, after_ref, out_ref):
        out_ref[...] = left_ref[...] + right_ref[...]

    return pl.pallas_call(
        kernel,
        in_specs=[WHOLE, WHOLE, ANYWHERE],
        out_specs=WHOLE,
        out_shape=pltpu.VMEM(left.shape, left.dtype),
        compiler_params=params(4),
        name="add_after",
    )(left, right, after)


def times_columns(total, pairs, end):
    columns, part = pairs[0][1].shape
    operands = [
        x
        for s, tall in pairs
        for x in (s, pltpu.with_memory_space_constraint(tall, pltpu.VMEM))
    ]
    if total is not None:
        operands.append(total)
    if end:
        out_shape = (
            jax.ShapeDtypeStruct((R, columns // 4 + LANES), F32),
            jax.ShapeDtypeStruct((R, columns // 4), F32),
        )
    else:
        out_shape = pltpu.VMEM((columns + 2 * R, 2 * R), F32)
    return pl.pallas_call(
        lambda *refs: columns_kernel(*refs, terms=len(pairs), begin=total is None, end=end),
        in_specs=[WHOLE] * len(operands),
        out_specs=(WHOLE, WHOLE) if end else WHOLE,
        out_shape=out_shape,
        compiler_params=params(12),
        cost_estimate=pl.CostEstimate(
            flops=4 * R * part * columns * len(pairs),
            bytes_accessed=2 * part * columns * len(pairs),
            transcendentals=0,
        ),
        name="times_columns",
    )(*operands)


def swap(value, axis, bit):
    size = lax.axis_size(axis)
    return lax.ppermute(value, axis, [(i, i ^ bit) for i in range(size)])


def sum_doubling(value, axis):
    bit = 1
    while bit < lax.axis_size(axis):
        value = value + swap(value, axis, bit)
        bit *= 2
    return value


def sum_both(left, right, axis, scaled):
    bits = []
    while 2 ** len(bits) < lax.axis_size(axis):
        bits.append(2 ** len(bits))
    for i in range(len(bits)):
        left_other = swap(left, axis, bits[i - 1])
        right_other = swap(right, axis, bits[i])
        left = left + left_other
        if i < len(bits) - 1:
            right = right + right_other
    inverse = pl.pallas_call(
        lambda *refs: factor_kernel(*refs, scaled=scaled),
        out_shape=jax.ShapeDtypeStruct((R, R), F32),
        compiler_params=params(4),
        name="factor",
    )(left)
    return inverse, left, add_after(right, right_other, inverse)


def sum_rest(value, axis, after):
    bit = 2
    while bit < lax.axis_size(axis):
        value = add_after(value, swap(value, axis, bit), after)
        bit *= 2
    return value


def shards(snapshots, sketch, sketch_next):
    rows = snapshots.shape[0]
    columns = snapshots.shape[1]
    rows_total = rows * lax.axis_size("space")
    kept_rows = {}

    for step in range(ITERS + 1):

        def role_rows(role, *after):
            if step:
                return times_rows(frame, kept_rows[role][0], after[0])
            s, *kept_rows[role] = first_rows(sketch.T, snapshots, role, after)
            return s

        if step:
            sent, frame = lead_rows(inverse, left, right, kept_rows[False, 0][0])
        else:
            sent = role_rows((False, 0))
        kept = role_rows((True, 0), sent)
        start = kept + swap(sent, "param", 1)
        sent = role_rows((False, 1), start)
        kept = role_rows((True, 1), sent)
        near = kept + swap(sent, "param", 1)
        start = sum_rest(start, "param", kept)
        full = [swap(start, "param", 1), start]
        talls = [kept_rows[role][1] for role in ROLES]
        total = times_columns(None, [(full[1], talls[1]), (full[0], talls[0])], False)
        near = sum_rest(near, "param", total)
        full += [swap(near, "param", 1), near]
        total = times_columns(total, [(full[3], talls[3])], False)
        left, right = times_columns(total, [(full[2], talls[2])], True)
        inverse, left, right = sum_both(left, right, "space", step < ITERS)
    width = N2 * N3
    local_next = columns // width * R
    basis, pieces, summed = pl.pallas_call(
        lambda *refs: last_kernel(*refs, rows_total=rows_total, roles=ROLES),
        out_shape=(
            jax.ShapeDtypeStruct((R, rows), F32),
            jax.ShapeDtypeStruct((R, local_next), F32),
            jax.ShapeDtypeStruct((R, width + LANES), F32),
        ),
        compiler_params=params(12),
        name="last",
    )(inverse, left, right, *full, sketch_next)
    summed = sum_doubling(summed, "param")
    next_rows = local_next * lax.axis_size("param")
    second, remainder = pl.pallas_call(
        lambda *refs: second_kernel(*refs, next_rows=next_rows),
        out_shape=(
            jax.ShapeDtypeStruct((R, local_next), F32),
            jax.ShapeDtypeStruct((R, width), F32),
        ),
        compiler_params=params(12),
        name="second",
    )(summed, pieces)
    return basis, second, remainder


def solution(mesh):
    placed = (P("space", "param"), P("param", None), P())
    return jax.shard_map(
        shards,
        mesh=mesh,
        in_specs=placed,
        out_specs=(P(None, "space"), P(None, "param"), P()),
        check_vma=False,
    )
```

```python
import math

import jax
import jax.numpy as jnp
from jax import lax
from jax.experimental import pallas as pl
from jax.experimental.pallas import tpu as pltpu
from jax.sharding import PartitionSpec as P

R = 32
N2 = 16
N3 = 16
ITERS = 3
HIGHEST = lax.Precision.HIGHEST
F32 = jnp.float32
BF16 = jnp.bfloat16
LANES = 128
NT = (((1,), (1,)), ((), ()))


def split(block):
    high = block.astype(BF16)
    return high, (block - high.astype(F32)).astype(BF16)


def stacked(block):
    return jnp.concatenate(split(block), axis=0)


def folded(product):
    turned = product.T
    return turned[:R] + turned[R:]


def first_row(keep, piece, rows):
    mine = lax.rem(lax.axis_index("param"), 2)
    half = mine if keep else 1 - mine
    return pl.multiple_of(half * (rows // 2) + piece * (rows // 4), LANES)


def keep_rows(a_ref, wide_refs, tall_ref, held, arrived, keep, piece, stored=None):
    slots, block, columns = held.shape
    part = tall_ref.shape[1]
    begin = first_row(keep, piece, a_ref.shape[0])
    copies = [
        pltpu.make_async_copy(
            a_ref.at[pl.ds(begin + i * block, block), :],
            held.at[i % slots],
            arrived.at[i % slots],
        )
        for i in range(part // block)
    ]
    leaving = []
    for copy in copies[:slots]:
        copy.start()
    for i, copy in enumerate(copies):
        copy.wait()
        at = i * block
        for half, value in enumerate(split(held[i % slots])):
            rows = slice(half * part + at, half * part + at + block)
            tall_ref[half * columns : (half + 1) * columns, at : at + block] = value.T
            for side, wide_ref in enumerate(wide_refs):
                wide_ref[rows, :] = value[:, side * columns // 2 : (side + 1) * columns // 2]
                if stored is not None:
                    leaving.append(
                        pltpu.make_async_copy(
                            wide_ref.at[rows, :],
                            stored[side].at[rows, :],
                            stored[2].at[4 * i + 2 * half + side],
                        )
                    )
                    leaving[-1].start()
        if i + slots < len(copies):
            copies[i + slots].start()
    return leaving


def rows_product(frame, wide_ref, part):
    product = lax.dot_general(wide_ref[...], frame, NT, preferred_element_type=F32)
    return product[:part] + product[part:]


def first_kernel(frame_ref, a_ref, *rest, keep, piece, after):
    out_ref, *stored, tall_ref, held, arrived = rest[after : after + 6]
    rest = rest[after + 6 :]
    wide_refs = rest[:2] or stored
    stored = (*stored, rest[2]) if rest else None
    leaving = keep_rows(a_ref, wide_refs, tall_ref, held, arrived, keep, piece, stored)
    frame = stacked(frame_ref[...])
    half = frame.shape[1] // 2
    part = out_ref.shape[1]
    product = rows_product(frame[:, :half], wide_refs[0], part)
    out_ref[...] = folded(product + rows_product(frame[:, half:], wide_refs[1], part))
    for copy in leaving:
        copy.wait()


def gram_of(left_ref):
    return left_ref[:, left_ref.shape[1] - LANES :][:, :R]


def diagonal(gram, axis):
    rows = lax.broadcasted_iota(jnp.int32, (R, R), 0)
    columns = lax.broadcasted_iota(jnp.int32, (R, R), 1)
    return jnp.sum(jnp.where(rows == columns, gram, 0.0), axis=axis, keepdims=True)


def rows_kernel(*refs, side, after):
    left_ref, *refs = refs
    source = left_ref if side == 0 else refs.pop(0)
    wide_ref, *refs = refs
    out_ref = refs[-1]
    part = out_ref.shape[1]
    scale = lax.rsqrt(diagonal(gram_of(left_ref), 1))
    frame = stacked(source[:, : wide_ref.shape[1]] * scale)
    out = folded(rows_product(frame, wide_ref, part))
    out_ref[...] = out + refs[0][...] if side else out


def columns_kernel(*refs, terms, factored, begin, side):
    refs = list(refs)
    inverse = refs.pop(0)[...] if factored else None
    sources, rest = refs[: 2 * terms], refs[2 * terms :]
    total_ref = None if begin else rest.pop(0)
    out_ref = rest[0]
    columns = sources[1].shape[0] // 2
    half = columns // 2
    if side is None:
        ranges = [slice(0, 2 * columns)]
    else:
        ranges = [slice(n, n + half) for n in (side * half, columns + side * half)]
    total = None
    if not begin:
        last = [] if side == 1 else [slice(2 * columns, 2 * columns + 2 * R)]
        total = jnp.concatenate([total_ref[at, :] for at in ranges + last], axis=0)
    for i in range(terms):
        s = sources[2 * i][...]
        if factored:
            s = jnp.dot(inverse, s, precision=HIGHEST, preferred_element_type=F32)
        s = stacked(s)
        tall_ref = sources[2 * i + 1]
        left = [tall_ref[at, :] for at in ranges] + ([] if side == 1 else [s])
        left = jnp.concatenate(left, axis=0)
        term = lax.dot_general(left, s, NT, preferred_element_type=F32)
        total = term if total is None else total + term
    if side is None:
        out_ref[...] = total
        return
    out_ref[:, :half] = folded(total[:half] + total[half:columns])
    if side == 0:
        both = total[columns:]
        gram = both[:R] + both[R:]
        out_ref[:, half:] = jnp.zeros((R, LANES), F32)
        out_ref[:, half : half + R] = gram[:, :R] + gram[:, R:]


def inverse_factor(gram):
    rows = lax.broadcasted_iota(jnp.int32, (R, LANES), 0)
    lanes = lax.broadcasted_iota(jnp.int32, (R, LANES), 1)
    state = gram + jnp.where(lanes == rows + R, 1.0, 0.0).astype(F32)
    scale = jnp.ones((R, 1), F32)
    for k in range(R):
        pivot = lax.rsqrt(state[k : k + 1, k : k + 1])
        row = state[k : k + 1, :] * pivot
        column = state[:, k : k + 1] * pivot
        below = state - column * row
        state = jnp.where(rows > k, below, jnp.where(rows == k, row, state))
        scale = jnp.where(rows[:, :1] == k, pivot, scale)
    return state[:, R : 2 * R], scale


def factor_kernel(left_ref, after_ref, out_ref, *, scaled):
    gram = gram_of(left_ref)
    by_row = lax.rsqrt(diagonal(gram, 1))
    by_column = lax.rsqrt(diagonal(gram, 0))
    even = jnp.concatenate([gram * by_row * by_column, jnp.zeros((R, LANES - R), F32)], axis=1)
    inverse, scale = inverse_factor(even)
    out_ref[...] = inverse * (scale * by_row) if scaled else inverse * by_column


def last_kernel(
    inverse_ref, before_ref, left_ref, right_ref, *refs, rows_total, roles
):
    s_refs, (next_ref, basis_ref, coefficients_ref, summed_ref) = refs[:-4], refs[-4:]
    half = right_ref.shape[1]
    product = jnp.concatenate([left_ref[:, :half], right_ref[...]], axis=1)
    columns = product.shape[1]
    inverse = inverse_ref[...]
    both = jnp.dot(inverse, before_ref[...], precision=HIGHEST, preferred_element_type=F32)
    for s_ref, (keep, piece) in zip(s_refs, roles):
        begin = first_row(keep, piece, basis_ref.shape[1])
        basis_ref[:, pl.ds(begin, s_ref.shape[1])] = jnp.dot(
            both, s_ref[...], precision=HIGHEST, preferred_element_type=F32
        ) * math.sqrt(rows_total)
    coefficients = jnp.dot(
        inverse, product, precision=HIGHEST, preferred_element_type=F32
    ) / math.sqrt(rows_total)
    width = N2 * N3
    modes = columns // width
    gram = jnp.zeros((R, R), F32)
    summed = jnp.zeros((R, width), F32)
    pieces = []
    for mode in range(modes):
        part = coefficients[:, mode * width : (mode + 1) * width]
        piece = lax.dot_general(
            next_ref[...], part, (((0,), (1,)), ((), ())), precision=HIGHEST,
            preferred_element_type=F32,
        )
        gram += lax.dot_general(piece, piece, NT, precision=HIGHEST, preferred_element_type=F32)
        summed += jnp.dot(piece, part, precision=HIGHEST, preferred_element_type=F32)
        pieces.append(piece)
    coefficients_ref[...] = jnp.concatenate(pieces, axis=1)
    gram = jnp.concatenate([gram, jnp.zeros((R, LANES - R), F32)], axis=1)
    summed_ref[...] = jnp.concatenate([summed, gram], axis=1)


def second_kernel(summed_ref, pieces_ref, frame_ref, remainder_ref, *, next_rows):
    width = N2 * N3
    inverse, _ = inverse_factor(summed_ref[:, width:])
    frame_ref[...] = jnp.dot(
        inverse, pieces_ref[...], precision=HIGHEST, preferred_element_type=F32
    ) * math.sqrt(next_rows)
    remainder_ref[...] = jnp.dot(
        inverse, summed_ref[:, :width], precision=HIGHEST, preferred_element_type=F32
    ) / math.sqrt(next_rows)


def params(mebibytes):
    return pltpu.CompilerParams(vmem_limit_bytes=mebibytes * 1024 * 1024)


WHOLE = pl.BlockSpec(memory_space=pltpu.VMEM)
ANYWHERE = pl.BlockSpec(memory_space=pl.ANY)


ROLES = ((False, 0), (True, 0), (False, 1), (True, 1))


COST = pl.CostEstimate(flops=1024, bytes_accessed=1024, transcendentals=0)


def first_rows(frame, a, role, after, block=256, slots=4):
    rows, columns = a.shape
    part = rows // 4
    a = pltpu.with_memory_space_constraint(a, pltpu.HBM)
    keep, piece = role
    wide = (2 * part, columns // 2)
    scratch = [pltpu.VMEM((slots, block, columns), F32), pltpu.SemaphoreType.DMA((slots,))]
    if piece:
        scratch += [pltpu.VMEM(wide, BF16)] * 2
        scratch.append(pltpu.SemaphoreType.DMA((4 * (part // block),)))
    return pl.pallas_call(
        lambda *refs: first_kernel(*refs, keep=keep, piece=piece, after=len(after)),
        in_specs=[WHOLE, pl.BlockSpec(memory_space=pltpu.HBM)] + [ANYWHERE] * len(after),
        out_specs=[WHOLE] + [pl.BlockSpec(memory_space=pltpu.HBM) if piece else WHOLE] * 2 + [WHOLE],
        out_shape=(
            pltpu.VMEM((R, part), F32),
            *[pltpu.HBM(wide, BF16) if piece else pltpu.VMEM(wide, BF16)] * 2,
            pltpu.VMEM((2 * columns, part), BF16),
        ),
        scratch_shapes=scratch,
        compiler_params=params(16 if piece else 10),
        cost_estimate=COST,
        name="first_rows",
    )(frame, a, *after)


def times_rows(left, right, partial, wide, after):
    part = wide.shape[0] // 2
    wide = pltpu.with_memory_space_constraint(wide, pltpu.VMEM)
    side = 0 if partial is None else 1
    operands = [left, right, wide, partial] if side else [left, wide]
    return pl.pallas_call(
        lambda *refs: rows_kernel(*refs, side=side, after=len(after)),
        in_specs=[WHOLE] * len(operands) + [ANYWHERE] * len(after),
        out_specs=WHOLE,
        out_shape=pltpu.VMEM((R, part), F32),
        compiler_params=params(12),
        cost_estimate=COST,
        name="times_rows",
    )(*operands, *after)


def add_after(left, right, after):
    def kernel(left_ref, right_ref, after_ref, out_ref):
        out_ref[...] = left_ref[...] + right_ref[...]

    return pl.pallas_call(
        kernel,
        in_specs=[WHOLE, WHOLE, ANYWHERE],
        out_specs=WHOLE,
        out_shape=pltpu.VMEM(left.shape, left.dtype),
        compiler_params=params(4),
        cost_estimate=COST,
        name="add_after",
    )(left, right, after)


def times_columns(inverse, total, pairs, side):
    columns, part = pairs[0][1].shape
    operands = [] if inverse is None else [inverse]
    for s, tall in pairs:
        operands += [s, pltpu.with_memory_space_constraint(tall, pltpu.VMEM)]
    if total is not None:
        operands.append(total)
    if side is None:
        out_shape = pltpu.VMEM((columns + 2 * R, 2 * R), F32)
    else:
        out_shape = jax.ShapeDtypeStruct((R, columns // 4 + (1 - side) * LANES), F32)
    return pl.pallas_call(
        lambda *refs: columns_kernel(
            *refs,
            terms=len(pairs),
            factored=inverse is not None,
            begin=total is None,
            side=side,
        ),
        in_specs=[WHOLE] * len(operands),
        out_specs=WHOLE,
        out_shape=out_shape,
        compiler_params=params(12),
        cost_estimate=COST,
        name="times_columns",
    )(*operands)


def swap(value, axis, bit):
    size = lax.axis_size(axis)
    return lax.ppermute(value, axis, [(i, i ^ bit) for i in range(size)])


def sum_doubling(value, axis):
    bit = 1
    while bit < lax.axis_size(axis):
        value = value + swap(value, axis, bit)
        bit *= 2
    return value


def factor(left, after, scaled):
    return pl.pallas_call(
        lambda *refs: factor_kernel(*refs, scaled=scaled),
        in_specs=[WHOLE, ANYWHERE],
        out_specs=WHOLE,
        out_shape=jax.ShapeDtypeStruct((R, R), F32),
        compiler_params=params(4),
        cost_estimate=COST,
        name="factor",
    )(left, after)


def bits_of(axis):
    bits = []
    while 2 ** len(bits) < lax.axis_size(axis):
        bits.append(2 ** len(bits))
    return bits


def sum_rest(value, axis, after):
    bit = 2
    while bit < lax.axis_size(axis):
        value = add_after(value, swap(value, axis, bit), after)
        bit *= 2
    return value


def shards(snapshots, sketch, sketch_next):
    rows = snapshots.shape[0]
    columns = snapshots.shape[1]
    rows_total = rows * lax.axis_size("space")
    kept_rows = {}
    inverse = left = right = None

    for step in range(ITERS + 1):
        partials = {}
        if step:
            after = ()
            for role in ROLES:
                partials[role] = times_rows(left, None, None, kept_rows[role][0], after)
                after = (partials[role],)
            right = add_after(right, right_other, after[0])

        def role_rows(role, *after):
            if step:
                return times_rows(left, right, partials[role], kept_rows[role][1], after)
            s, *kept_rows[role] = first_rows(sketch.T, snapshots, role, after)
            return s

        sent = role_rows((False, 0))
        kept = role_rows((True, 0), sent)
        start = kept + swap(sent, "param", 1)
        sent = role_rows((False, 1), start)
        kept = role_rows((True, 1), sent)
        near = kept + swap(sent, "param", 1)
        if step:
            inverse = factor(left, near, True)
        start = sum_rest(start, "param", inverse if step else near)
        full = [swap(start, "param", 1), start]
        talls = [kept_rows[role][2] for role in ROLES]
        total = times_columns(inverse, None, [(full[1], talls[1]), (full[0], talls[0])], None)
        near = sum_rest(near, "param", total)
        full += [swap(near, "param", 1), near]
        total = times_columns(inverse, total, [(full[3], talls[3])], None)
        left = times_columns(inverse, total, [(full[2], talls[2])], 0)
        right = times_columns(inverse, total, [(full[2], talls[2])], 1)
        bits = bits_of("space")
        for bit in bits[:-1]:
            left = add_after(left, swap(left, "space", bit), right)
            right = right + swap(right, "space", bit)
        left = left + swap(left, "space", bits[-1])
        right_other = swap(right, "space", bits[-1])
    before = inverse
    inverse = factor(left, left, False)
    right = add_after(right, right_other, inverse)
    width = N2 * N3
    local_next = columns // width * R
    basis, pieces, summed = pl.pallas_call(
        lambda *refs: last_kernel(*refs, rows_total=rows_total, roles=ROLES),
        out_shape=(
            jax.ShapeDtypeStruct((R, rows), F32),
            jax.ShapeDtypeStruct((R, local_next), F32),
            jax.ShapeDtypeStruct((R, width + LANES), F32),
        ),
        compiler_params=params(12),
        name="last",
    )(inverse, before, left, right, *full, sketch_next)
    summed = sum_doubling(summed, "param")
    next_rows = local_next * lax.axis_size("param")
    second, remainder = pl.pallas_call(
        lambda *refs: second_kernel(*refs, next_rows=next_rows),
        out_shape=(
            jax.ShapeDtypeStruct((R, local_next), F32),
            jax.ShapeDtypeStruct((R, width), F32),
        ),
        compiler_params=params(12),
        name="second",
    )(summed, pieces)
    return basis, second, remainder


def solution(mesh):
    placed = (P("space", "param"), P("param", None), P())
    return jax.shard_map(
        shards,
        mesh=mesh,
        in_specs=placed,
        out_specs=(P(None, "space"), P(None, "param"), P()),
        check_vma=False,
    )
```

```python
import math

import jax
import jax.numpy as jnp
from jax import lax
from jax.experimental import pallas as pl
from jax.experimental.pallas import tpu as pltpu
from jax.sharding import PartitionSpec as P

R = 32
N2 = 16
N3 = 16
ITERS = 3
HIGHEST = lax.Precision.HIGHEST
F32 = jnp.float32
BF16 = jnp.bfloat16
LANES = 128
NT = (((1,), (1,)), ((), ()))


def split(block):
    high = block.astype(BF16)
    return high, (block - high.astype(F32)).astype(BF16)


def stacked(block):
    return jnp.concatenate(split(block), axis=0)


def folded(product):
    turned = product.T
    return turned[:R] + turned[R:]


def first_row(keep, piece, rows):
    mine = lax.rem(lax.axis_index("param"), 2)
    half = mine if keep else 1 - mine
    return pl.multiple_of(half * (rows // 2) + piece * (rows // 4), LANES)


def first_kernel(frame_ref, a_ref, *rest, keep, piece, after):
    out_ref, stored_ref, tall_ref, held, arrived, *rest = rest[after:]
    wide_ref, *sent = rest or [stored_ref]
    blocks, block, columns = held.shape
    part = out_ref.shape[1]
    begin = first_row(keep, piece, a_ref.shape[0])
    frame = stacked(frame_ref[...])

    def coming(i):
        rows = pl.ds(begin + pl.multiple_of(i * block, block), block)
        return pltpu.make_async_copy(a_ref.at[rows, :], held.at[i], arrived.at[i])

    def leaving(i, half):
        rows = pl.ds(pl.multiple_of(half * part + i * block, block), block)
        return pltpu.make_async_copy(
            wide_ref.at[rows, :], stored_ref.at[rows, :], sent[0].at[2 * i + half]
        )

    for i in range(blocks):
        coming(i).start()

    def body(i, carry):
        at = pl.ds(pl.multiple_of(i * block, block), block)
        coming(i).wait()
        parts = split(held[i])
        for half, value in enumerate(parts):
            wide_ref[pl.ds(pl.multiple_of(half * part + i * block, block), block), :] = value
            tall_ref[half * columns : (half + 1) * columns, at] = value.T
            if sent:
                leaving(i, half).start()
        product = lax.dot_general(
            jnp.concatenate(parts, axis=0), frame, NT, preferred_element_type=F32
        )
        out_ref[:, at] = folded(product[:block] + product[block:])
        return carry

    lax.fori_loop(0, blocks, body, 0)
    if sent:
        for i in range(blocks):
            for half in range(2):
                leaving(i, half).wait()


def gram_of(left_ref):
    return left_ref[:, left_ref.shape[1] - LANES :][:, :R]


def diagonal(gram, axis):
    rows = lax.broadcasted_iota(jnp.int32, (R, R), 0)
    columns = lax.broadcasted_iota(jnp.int32, (R, R), 1)
    return jnp.sum(jnp.where(rows == columns, gram, 0.0), axis=axis, keepdims=True)


def rows_kernel(left_ref, right_ref, wide_ref, *rest, after, block):
    out_ref, frame_ref, sum_ref = rest[after:]
    part = out_ref.shape[1]
    half = right_ref.shape[1]
    scale = lax.rsqrt(diagonal(gram_of(left_ref), 1))
    frame_ref[:, :half] = stacked(left_ref[:, :half] * scale)
    frame_ref[:, half:] = stacked(right_ref[...] * scale)
    sum_ref[...] = jnp.zeros_like(sum_ref)

    def body(i, carry):
        at = pl.ds(pl.multiple_of(i * block, block), block)
        sum_ref[...] += lax.dot_general(
            wide_ref[:, at], frame_ref[:, at], NT, preferred_element_type=F32
        )
        return carry

    lax.fori_loop(0, 2 * half // block, body, 0)
    out_ref[...] = folded(sum_ref[:part] + sum_ref[part:])


def columns_kernel(*refs, terms, factored, begin, end, block):
    refs = list(refs)
    inverse = refs.pop(0)[...] if factored else None
    sources, rest = refs[: 2 * terms], refs[2 * terms :]
    total_ref = None if begin else rest.pop(0)
    sum_ref = rest[-1]
    columns = sources[1].shape[0] // 2
    half = columns // 2
    sum_ref[...] = jnp.zeros_like(sum_ref) if begin else total_ref[...]
    for s_ref, tall_ref in zip(sources[::2], sources[1::2]):

        def body(i, carry):
            at = pl.ds(pl.multiple_of(i * block, block), block)
            s = s_ref[:, at]
            if factored:
                s = jnp.dot(inverse, s, precision=HIGHEST, preferred_element_type=F32)
            s = stacked(s)
            left = jnp.concatenate([tall_ref[:, at], s], axis=0)
            sum_ref[...] += lax.dot_general(left, s, NT, preferred_element_type=F32)
            return carry

        lax.fori_loop(0, s_ref.shape[1] // block, body, 0)
    if not end:
        return
    left_ref, right_ref = rest[:2]
    product = folded(sum_ref[:columns] + sum_ref[columns : 2 * columns])
    both = sum_ref[2 * columns :]
    gram = both[:R] + both[R:]
    left_ref[:, :half] = product[:, :half]
    left_ref[:, half:] = jnp.zeros((R, LANES), F32)
    left_ref[:, half : half + R] = gram[:, :R] + gram[:, R:]
    right_ref[...] = product[:, half:]


def inverse_factor(gram):
    rows = lax.broadcasted_iota(jnp.int32, (R, LANES), 0)
    lanes = lax.broadcasted_iota(jnp.int32, (R, LANES), 1)
    state = gram + jnp.where(lanes == rows + R, 1.0, 0.0).astype(F32)
    scale = jnp.ones((R, 1), F32)
    for k in range(R):
        pivot = lax.rsqrt(state[k : k + 1, k : k + 1])
        row = state[k : k + 1, :] * pivot
        column = state[:, k : k + 1] * pivot
        below = state - column * row
        state = jnp.where(rows > k, below, jnp.where(rows == k, row, state))
        scale = jnp.where(rows[:, :1] == k, pivot, scale)
    return state[:, R : 2 * R], scale


def factor_kernel(left_ref, after_ref, out_ref, *, scaled):
    gram = gram_of(left_ref)
    by_row = lax.rsqrt(diagonal(gram, 1))
    by_column = lax.rsqrt(diagonal(gram, 0))
    even = jnp.concatenate([gram * by_row * by_column, jnp.zeros((R, LANES - R), F32)], axis=1)
    inverse, scale = inverse_factor(even)
    out_ref[...] = inverse * (scale * by_row) if scaled else inverse * by_column


def last_kernel(
    inverse_ref, before_ref, left_ref, right_ref, *refs, rows_total, roles
):
    s_refs, (next_ref, basis_ref, coefficients_ref, summed_ref) = refs[:-4], refs[-4:]
    half = right_ref.shape[1]
    product = jnp.concatenate([left_ref[:, :half], right_ref[...]], axis=1)
    columns = product.shape[1]
    inverse = inverse_ref[...]
    both = jnp.dot(inverse, before_ref[...], precision=HIGHEST, preferred_element_type=F32)
    for s_ref, (keep, piece) in zip(s_refs, roles):
        begin = first_row(keep, piece, basis_ref.shape[1])
        basis_ref[:, pl.ds(begin, s_ref.shape[1])] = jnp.dot(
            both, s_ref[...], precision=HIGHEST, preferred_element_type=F32
        ) * math.sqrt(rows_total)
    coefficients = jnp.dot(
        inverse, product, precision=HIGHEST, preferred_element_type=F32
    ) / math.sqrt(rows_total)
    width = N2 * N3
    modes = columns // width
    gram = jnp.zeros((R, R), F32)
    summed = jnp.zeros((R, width), F32)
    pieces = []
    for mode in range(modes):
        part = coefficients[:, mode * width : (mode + 1) * width]
        piece = lax.dot_general(
            next_ref[...], part, (((0,), (1,)), ((), ())), precision=HIGHEST,
            preferred_element_type=F32,
        )
        gram += lax.dot_general(piece, piece, NT, precision=HIGHEST, preferred_element_type=F32)
        summed += jnp.dot(piece, part, precision=HIGHEST, preferred_element_type=F32)
        pieces.append(piece)
    coefficients_ref[...] = jnp.concatenate(pieces, axis=1)
    gram = jnp.concatenate([gram, jnp.zeros((R, LANES - R), F32)], axis=1)
    summed_ref[...] = jnp.concatenate([summed, gram], axis=1)


def second_kernel(summed_ref, pieces_ref, frame_ref, remainder_ref, *, next_rows):
    width = N2 * N3
    inverse, _ = inverse_factor(summed_ref[:, width:])
    frame_ref[...] = jnp.dot(
        inverse, pieces_ref[...], precision=HIGHEST, preferred_element_type=F32
    ) * math.sqrt(next_rows)
    remainder_ref[...] = jnp.dot(
        inverse, summed_ref[:, :width], precision=HIGHEST, preferred_element_type=F32
    ) / math.sqrt(next_rows)


def params(mebibytes):
    return pltpu.CompilerParams(vmem_limit_bytes=mebibytes * 1024 * 1024)


WHOLE = pl.BlockSpec(memory_space=pltpu.VMEM)
ANYWHERE = pl.BlockSpec(memory_space=pl.ANY)


ROLES = ((False, 0), (True, 0), (False, 1), (True, 1))


COST = pl.CostEstimate(flops=1024, bytes_accessed=1024, transcendentals=0)


def first_rows(frame, a, role, after, block=512):
    rows, columns = a.shape
    part = rows // 4
    a = pltpu.with_memory_space_constraint(a, pltpu.HBM)
    keep, piece = role
    wide = (2 * part, columns)
    blocks = part // block
    scratch = [pltpu.VMEM((blocks, block, columns), F32), pltpu.SemaphoreType.DMA((blocks,))]
    if piece:
        scratch += [pltpu.VMEM(wide, BF16), pltpu.SemaphoreType.DMA((2 * blocks,))]
    return pl.pallas_call(
        lambda *refs: first_kernel(*refs, keep=keep, piece=piece, after=len(after)),
        in_specs=[WHOLE, pl.BlockSpec(memory_space=pltpu.HBM)] + [ANYWHERE] * len(after),
        out_specs=[WHOLE, pl.BlockSpec(memory_space=pltpu.HBM) if piece else WHOLE, WHOLE],
        out_shape=(
            pltpu.VMEM((R, part), F32),
            pltpu.HBM(wide, BF16) if piece else pltpu.VMEM(wide, BF16),
            pltpu.VMEM((2 * columns, part), BF16),
        ),
        scratch_shapes=scratch,
        compiler_params=params(18 if piece else 12),
        cost_estimate=COST,
        name="first_rows",
    )(frame, a, *after)


def times_rows(left, right, wide, after, block=512):
    part, columns = wide.shape[0] // 2, wide.shape[1]
    wide = pltpu.with_memory_space_constraint(wide, pltpu.VMEM)
    return pl.pallas_call(
        lambda *refs: rows_kernel(*refs, after=len(after), block=block),
        in_specs=[WHOLE] * 3 + [ANYWHERE] * len(after),
        out_specs=WHOLE,
        out_shape=pltpu.VMEM((R, part), F32),
        scratch_shapes=[
            pltpu.VMEM((2 * R, columns), BF16),
            pltpu.VMEM((2 * part, 2 * R), F32),
        ],
        compiler_params=params(12),
        cost_estimate=COST,
        name="times_rows",
    )(left, right, wide, *after)


def add_after(left, right, after):
    def kernel(left_ref, right_ref, after_ref, out_ref):
        out_ref[...] = left_ref[...] + right_ref[...]

    return pl.pallas_call(
        kernel,
        in_specs=[WHOLE, WHOLE, ANYWHERE],
        out_specs=WHOLE,
        out_shape=pltpu.VMEM(left.shape, left.dtype),
        compiler_params=params(4),
        cost_estimate=COST,
        name="add_after",
    )(left, right, after)


def times_columns(inverse, total, pairs, end, block=512):
    columns, part = pairs[0][1].shape
    operands = [] if inverse is None else [inverse]
    for s, tall in pairs:
        operands += [s, pltpu.with_memory_space_constraint(tall, pltpu.VMEM)]
    if total is not None:
        operands.append(total)
    sums = pltpu.VMEM((columns + 2 * R, 2 * R), F32)
    if end:
        out_shape = (
            jax.ShapeDtypeStruct((R, columns // 4 + LANES), F32),
            jax.ShapeDtypeStruct((R, columns // 4), F32),
        )
    else:
        out_shape = sums
    return pl.pallas_call(
        lambda *refs: columns_kernel(
            *refs,
            terms=len(pairs),
            factored=inverse is not None,
            begin=total is None,
            end=end,
            block=block,
        ),
        in_specs=[WHOLE] * len(operands),
        out_specs=(WHOLE, WHOLE) if end else WHOLE,
        out_shape=out_shape,
        scratch_shapes=[sums] if end else [],
        compiler_params=params(12),
        cost_estimate=COST,
        name="times_columns",
    )(*operands)


def swap(value, axis, bit):
    size = lax.axis_size(axis)
    return lax.ppermute(value, axis, [(i, i ^ bit) for i in range(size)])


def sum_doubling(value, axis):
    bit = 1
    while bit < lax.axis_size(axis):
        value = value + swap(value, axis, bit)
        bit *= 2
    return value


def factor(left, after, scaled):
    return pl.pallas_call(
        lambda *refs: factor_kernel(*refs, scaled=scaled),
        in_specs=[WHOLE, ANYWHERE],
        out_specs=WHOLE,
        out_shape=jax.ShapeDtypeStruct((R, R), F32),
        compiler_params=params(4),
        cost_estimate=COST,
        name="factor",
    )(left, after)


def sum_both(left, right, axis):
    bits = []
    while 2 ** len(bits) < lax.axis_size(axis):
        bits.append(2 ** len(bits))
    for i in range(len(bits)):
        left_other = swap(left, axis, bits[i])
        right_other = swap(right, axis, bits[i - 1])
        left = left + left_other
        right = right + right_other
    return left, right


def sum_rest(value, axis, after):
    bit = 2
    while bit < lax.axis_size(axis):
        value = add_after(value, swap(value, axis, bit), after)
        bit *= 2
    return value


def shards(snapshots, sketch, sketch_next):
    rows = snapshots.shape[0]
    columns = snapshots.shape[1]
    rows_total = rows * lax.axis_size("space")
    kept_rows = {}
    inverse = left = right = None

    for step in range(ITERS + 1):

        def role_rows(role, *after):
            if step:
                return times_rows(left, right, kept_rows[role][0], after)
            s, *kept_rows[role] = first_rows(sketch.T, snapshots, role, after)
            return s

        sent = role_rows((False, 0))
        kept = role_rows((True, 0), sent)
        start = kept + swap(sent, "param", 1)
        sent = role_rows((False, 1), start)
        kept = role_rows((True, 1), sent)
        near = kept + swap(sent, "param", 1)
        start = sum_rest(start, "param", kept)
        if step:
            inverse = factor(left, start, True)
        full = [swap(start, "param", 1), start]
        talls = [kept_rows[role][1] for role in ROLES]
        total = times_columns(inverse, None, [(full[1], talls[1]), (full[0], talls[0])], False)
        near = sum_rest(near, "param", total)
        full += [swap(near, "param", 1), near]
        total = times_columns(inverse, total, [(full[3], talls[3])], False)
        left, right = times_columns(inverse, total, [(full[2], talls[2])], True)
        left, right = sum_both(left, right, "space")
    before = inverse
    inverse = factor(left, left, False)
    width = N2 * N3
    local_next = columns // width * R
    basis, pieces, summed = pl.pallas_call(
        lambda *refs: last_kernel(*refs, rows_total=rows_total, roles=ROLES),
        out_shape=(
            jax.ShapeDtypeStruct((R, rows), F32),
            jax.ShapeDtypeStruct((R, local_next), F32),
            jax.ShapeDtypeStruct((R, width + LANES), F32),
        ),
        compiler_params=params(12),
        name="last",
    )(inverse, before, left, right, *full, sketch_next)
    summed = sum_doubling(summed, "param")
    next_rows = local_next * lax.axis_size("param")
    second, remainder = pl.pallas_call(
        lambda *refs: second_kernel(*refs, next_rows=next_rows),
        out_shape=(
            jax.ShapeDtypeStruct((R, local_next), F32),
            jax.ShapeDtypeStruct((R, width), F32),
        ),
        compiler_params=params(12),
        name="second",
    )(summed, pieces)
    return basis, second, remainder


def solution(mesh):
    placed = (P("space", "param"), P("param", None), P())
    return jax.shard_map(
        shards,
        mesh=mesh,
        in_specs=placed,
        out_specs=(P(None, "space"), P(None, "param"), P()),
        check_vma=False,
    )
```
